32 devices in a mesh: fsdp: 16 (over z, y, x), tp: 2 (over core).
Axes of the slice: x: 2, y: 2, z: 4, core: 2. Of those that a mesh axis runs over, the one named last changes fastest.
Arguments:
- activations: bfloat16 [256, 18432], P('fsdp', 'tp'), may hold values from -6 to 6
- down_weight: bfloat16 [4608, 18432], P('fsdp', 'tp'), may hold values from -0.046875 to 0.046875
- basis: bfloat16 [8, 4608, 18432], P(None, 'fsdp', 'tp'), may hold values from -64 to 64, as said below
- target: bfloat16 [4608, 256], P('fsdp'), may hold values from -6 to 6
Outputs:
- new_vector: float32 [4608, 18432], P('fsdp', 'tp')
- hessenberg: float32 [9], replicated
The draws below stay inside these ranges and needn't reach their ends.
Inputs may be any that keep to these rules, and one draw needn't show every extreme that they name: The basis vectors are linearly independent and not orthogonal.
All inputs are finite; a program needn't handle non-finite values.
Results may differ from the reference program's by a relative error of at most 0.00055.
Values may be sent and summed in bfloat16 or wider, within the bound.
A program may use at most 256 MiB of HBM per device.

```python
import math
import jax
import jax.numpy as jnp
from jax import lax

D = 4608
FFW = 18432
K = 8
TOKENS = 256


def draw_basis(key, part):
    key = jax.random.fold_in(key, 11)
    keys = jax.random.split(key, 7)
    own = jax.random.truncated_normal(keys[0], -4.0, 4.0, (K, D, FFW), jnp.float32)
    shared = jax.random.truncated_normal(keys[1], -4.0, 4.0, (D, FFW), jnp.float32)
    rising = jnp.exp(math.log(3.0) * (jnp.arange(D, dtype=jnp.float32) / D - 0.5))[:, None]
    row_factor = rising * jnp.exp(jax.random.uniform(keys[2], (D, 1), jnp.float32, math.log(0.6), math.log(1.7)))
    phase = jax.random.randint(keys[6], (), 0, 2)
    heavy = (jnp.arange(FFW, dtype=jnp.int32) + phase) % 2
    alternate = jnp.where(heavy == 1, 1.8, 0.55).astype(jnp.float32)[None, :]
    col_factor = alternate * jnp.exp(jax.random.uniform(keys[3], (1, FFW), jnp.float32, math.log(0.6), math.log(1.6)))
    mixing = jax.random.uniform(keys[4], (K, 1, 1), jnp.float32, 0.15, 0.95)
    amplitude = jnp.exp(jax.random.uniform(keys[5], (K, 1, 1), jnp.float32, math.log(0.7), math.log(1.3)))
    combined = mixing * shared[None] + jnp.sqrt(1.0 - mixing * mixing) * own
    return (amplitude * combined * row_factor * col_factor).astype(jnp.bfloat16)


def block_levels(own_key, dims, shards, least, top_value):
    loudness = 1.0
    for position, blocks in shards:
        draws = jax.random.uniform(jax.random.fold_in(jax.random.fold_in(own_key, 6), position), (blocks,), jnp.float32, least / len(shards), top_value / len(shards))
        loudness = loudness * jnp.repeat(jnp.exp(draws), dims[position] // blocks).reshape((-1,) + (1,) * (len(dims) - 1 - position))
    return loudness


def scatter_about(own_key, dims, spread, limit, pieces=(), kind=jnp.bfloat16):
    loudness = block_levels(own_key, dims, pieces, -0.22, 0.18) if pieces else 1.0
    drawn = jax.random.normal(own_key, dims, jnp.float32) * spread * loudness
    return jnp.minimum(jnp.maximum(drawn, -limit), limit).astype(kind)


def setup_inputs(seed: int = 0) -> dict:
    arg_keys = jax.random.split(jax.random.key(seed), 5)
    activations = scatter_about(arg_keys[0], (TOKENS, FFW), 1.0, 6.0, ((0, 16), (1, 2)))
    down_weight = scatter_about(arg_keys[1], (D, FFW), FFW ** -0.5, 0.046875, ((0, 16), (1, 2)))
    basis = draw_basis(jax.random.fold_in(arg_keys[4], 71), 0)
    target = scatter_about(arg_keys[3], (D, TOKENS), 1.5, 6.0, ((0, 16),))
    return dict(activations=activations, down_weight=down_weight, basis=basis, target=target)


def inner_all(basis, field):
    count = float(D * FFW)
    return lax.map(lambda vector: jnp.sum(vector.astype(jnp.float32) * field), basis) / count

def remove_span(basis, coeffs, field):

    def step(acc, pair):
        vector, weight = pair
        return (acc - weight * vector.astype(jnp.float32), None)
    return lax.scan(step, field, (basis, coeffs))[0]

def reference(activations, down_weight, basis, target):
    direction = basis[K - 1]
    both = jnp.concatenate([down_weight, direction], 0)
    proj = lax.dot_general(both, activations, (((1,), (1,)), ((), ())), preferred_element_type=jnp.float32)
    outputs = proj[:D]
    tangent = proj[D:]
    resid = outputs - target.astype(jnp.float32)
    slope = jnp.tanh(resid)
    curvature = 1.0 - slope * slope
    weighted = (curvature * tangent).astype(jnp.bfloat16)
    hvp = jnp.dot(weighted, activations, preferred_element_type=jnp.float32) / float(TOKENS)
    first = inner_all(basis, hvp)
    once = remove_span(basis, first, hvp)
    second = inner_all(basis, once)
    twice = remove_span(basis, second, once)
    beta = jnp.sqrt(jnp.sum(twice * twice) / float(D * FFW))
    new_vector = twice / beta
    hessenberg = jnp.concatenate([first + second, beta[None]])
    return (new_vector, hessenberg)
```

```python
import functools
import jax
import jax.numpy as jnp
from jax import lax
from jax.experimental import pallas as pl
from jax.experimental.pallas import tpu as pltpu
from jax.sharding import PartitionSpec as P

D = 4608
FFW = 18432
MESH = pl.DeviceIdType.MESH
NT = (((1,), (1,)), ((), ()))
CHUNK = 1024
HALF = CHUNK // 2
GROUP = 32
LAG = 2


def plain_body(activations, down_weight, basis, target):
    count = float(D * FFW)
    total_tokens = target.shape[1]
    local_rows = down_weight.shape[0]
    basis_count = basis.shape[0]
    basis_flat = basis.reshape(basis_count, -1)
    gram = (
        lax.psum(
            lax.dot_general(
                basis_flat, basis_flat, (((1,), (1,)), ((), ())), preferred_element_type=jnp.float32
            ),
            ("fsdp", "tp"),
        )
        / count
    )
    both = jnp.concatenate([down_weight, basis[basis_count - 1]], 0)
    proj = lax.dot_general(
        both,
        lax.all_gather(activations, "fsdp", axis=0, tiled=True),
        (((1,), (1,)), ((), ())),
        preferred_element_type=jnp.float32,
    )
    summed = lax.psum(proj, "tp")
    slope = jnp.tanh(summed[:local_rows] - target.astype(jnp.float32))
    weighted = ((1.0 - slope * slope) * summed[local_rows:]).astype(jnp.bfloat16)
    hvp = jnp.dot(
        weighted,
        lax.all_gather(activations, "fsdp", axis=0, tiled=True),
        preferred_element_type=jnp.float32,
    ) / float(total_tokens)
    flat = hvp.reshape(1, -1)
    upper = flat.astype(jnp.bfloat16)
    lower = (flat - upper.astype(jnp.float32)).astype(jnp.bfloat16)
    panel = jnp.concatenate([upper, lower], 0)
    pairs = lax.dot_general(
        basis_flat, panel, (((1,), (1,)), ((), ())), preferred_element_type=jnp.float32
    )
    products, total_sq = lax.psum((jnp.sum(pairs, axis=1), jnp.sum(hvp * hvp)), ("fsdp", "tp"))
    products = products / count
    total_sq = total_sq / count
    second = products - jnp.dot(gram, products, precision=lax.Precision.HIGHEST)
    coeffs = products + second
    result = hvp
    for index in range(basis_count):
        result = result - coeffs[index] * basis[index].astype(jnp.float32)
    squares = (
        total_sq
        - 2.0 * jnp.sum(coeffs * products)
        + jnp.sum(coeffs * jnp.dot(gram, coeffs, precision=lax.Precision.HIGHEST))
    )
    beta = jnp.sqrt(squares)
    new_vector = result / beta
    hessenberg = jnp.concatenate([products + second, beta[None]])
    return (new_vector, hessenberg)


def gather_kernel(
    steps, act_hbm, w_hbm, basis_hbm, target_ref,
    act_out, weighted_out, coef_out,
    stack, held, proj, gram, tokgram, other, cur, got, zslots,
    own_sem, load_w, load_b, z_send, z_recv, s2, r2, s3, r3, out_sem,
    ex_send, ex_recv, red_send, red_recv,
):
    me = lax.axis_index("fsdp")
    core = lax.axis_index("tp")
    mz, my, mx = me // 4, (me // 2) % 2, me % 2
    xnb = {"fsdp": mz * 4 + my * 2 + (1 - mx)}
    ynb = {"fsdp": mz * 4 + (1 - my) * 2 + mx}
    tnb = {"tp": 1 - core}
    rows = w_hbm.shape[0]
    kb = basis_hbm.shape[0]

    def znb(shift):
        return {"fsdp": lax.rem(mz + shift, 4) * 4 + my * 2 + mx}

    def cols(t, start=0, size=CHUNK):
        return pl.ds(pl.multiple_of(t * CHUNK + start, HALF), size)

    own = pltpu.make_async_copy(act_hbm, held.at[mz, my, mx], own_sem)
    own.start()

    def copy_w(t):
        return pltpu.make_async_copy(w_hbm.at[:, cols(t)], stack.at[0, :, cols(t)], load_w.at[t])

    def copy_b(t):
        return pltpu.make_async_copy(
            basis_hbm.at[:, :, cols(t)], stack.at[pl.ds(1, kb), :, cols(t)], load_b.at[t]
        )

    @pl.loop(0, steps)
    def _(t):
        copy_w(t).start()
        copy_b(t).start()

    barrier = pltpu.get_barrier_semaphore()
    for nb in (znb(1), znb(2), znb(3), xnb, ynb, tnb):
        pl.semaphore_signal(barrier, inc=1, device_id=nb, device_id_type=MESH)
    proj[...] = jnp.zeros_like(proj)
    gram[...] = jnp.zeros_like(gram)
    tokgram[...] = jnp.zeros_like(tokgram)
    pl.semaphore_wait(barrier, 6)
    own.wait()

    def copy_z(t, shift, arriving):
        z = lax.rem(mz + 4 - shift, 4) if arriving else mz
        part = held.at[z, my, mx, :, cols(t)]
        return pltpu.make_async_remote_copy(
            part, part, z_send.at[t, shift - 1], z_recv.at[t, shift - 1],
            device_id=znb(shift), device_id_type=MESH,
        )

    def copy_2(t, way, arriving):
        if way == 0:
            part = held.at[:, my, (1 - mx) if arriving else mx, :, cols(t, 0, HALF)]
        else:
            part = held.at[:, (1 - my) if arriving else my, mx, :, cols(t, HALF, HALF)]
        return pltpu.make_async_remote_copy(
            part, part, s2.at[way, t], r2.at[way, t],
            device_id=xnb if way == 0 else ynb, device_id_type=MESH,
        )

    def copy_3(t, way, arriving):
        if way == 0:
            part = held.at[:, (1 - my) if arriving else my, :, :, cols(t, 0, HALF)]
        else:
            part = held.at[:, :, (1 - mx) if arriving else mx, :, cols(t, HALF, HALF)]
        return pltpu.make_async_remote_copy(
            part, part, s3.at[way, t], r3.at[way, t],
            device_id=ynb if way == 0 else xnb, device_id_type=MESH,
        )

    def copy_out(t):
        return pltpu.make_async_copy(
            held.at[:, :, :, :, cols(t)], act_out.at[:, :, :, :, cols(t)], out_sem.at[t]
        )

    @pl.loop(0, steps)
    def _(t):
        for shift in (1, 2, 3):
            copy_z(t, shift, False).start()

    @pl.loop(0, steps + 2 * LAG)
    def _(t):
        @pl.when(t < steps)
        def _():
            for shift in (1, 2, 3):
                copy_z(t, shift, True).wait_recv()
            copy_2(t, 0, False).start()
            copy_2(t, 1, False).start()

        @pl.when((t >= LAG) & (t < steps + LAG))
        def _():
            u = t - LAG
            for way in (0, 1):
                copy_2(u, way, True).wait_recv()
                copy_3(u, way, False).start()

        @pl.when(t < steps)
        def _():
            copy_w(t).wait()
            copy_b(t).wait()

            @pl.loop(0, rows // GROUP)
            def _(g):
                at = pl.ds(pl.multiple_of(g * GROUP, GROUP), GROUP)
                part = stack[1:, at, cols(t)].reshape(kb * GROUP, CHUNK)
                gram[...] += lax.dot_general(part, part, NT, preferred_element_type=jnp.float32)

        @pl.when(t >= 2 * LAG)
        def _():
            u = t - 2 * LAG
            copy_3(u, 0, True).wait_recv()
            copy_3(u, 1, True).wait_recv()
            copy_out(u).start()
            act = held[:, :, :, :, cols(u)].reshape(proj.shape[2], CHUNK)
            tokgram[...] += lax.dot_general(act, act, NT, preferred_element_type=jnp.float32)

            @pl.loop(0, rows // GROUP)
            def _(g):
                at = pl.ds(pl.multiple_of(g * GROUP, GROUP), GROUP)
                part = stack[:, at, cols(u)].reshape((kb + 1) * GROUP, CHUNK)
                act = held[:, :, :, :, cols(u)].reshape(proj.shape[2], CHUNK)
                made = lax.dot_general(part, act, NT, preferred_element_type=jnp.float32)
                proj[:, at, :] += made.reshape(kb + 1, GROUP, proj.shape[2])

    exchange = [
        pltpu.make_async_remote_copy(
            proj.at[k], other.at[i], ex_send.at[i], ex_recv.at[i],
            device_id=tnb, device_id_type=MESH,
        )
        for i, k in enumerate((0, kb))
    ]
    for copy in exchange:
        copy.start()

    lane = lax.broadcasted_iota(jnp.int32, (8, 128), 1)
    row = lax.broadcasted_iota(jnp.int32, (8, 128), 0)
    size = kb * GROUP
    r_at = lax.broadcasted_iota(jnp.int32, (size, size), 0)
    c_at = lax.broadcasted_iota(jnp.int32, (size, size), 1)
    kept = jnp.where(r_at % GROUP == c_at % GROUP, gram[...], 0.0)
    sums = jnp.sum(kept.reshape(kb, GROUP, size), axis=1)
    block = lax.broadcasted_iota(jnp.int32, (kb, size), 1) // GROUP
    tile = jnp.zeros((8, 128), jnp.float32)
    for k in range(kb):
        one = jnp.sum(jnp.where(block == k, sums, 0.0), axis=1, keepdims=True)
        tile = jnp.where(lane == k, one, tile)

    for copy in exchange:
        copy.wait()
    slope = jnp.tanh(proj[0] + other[0] - target_ref[...].astype(jnp.float32))
    weighted = ((1.0 - slope * slope) * (proj[kb] + other[1])).astype(jnp.bfloat16)
    weighted_out[...] = weighted
    wide = weighted.astype(jnp.float32)
    for k in range(kb):
        one = jnp.sum(jnp.sum(wide * proj[k + 1], axis=0, keepdims=True), axis=1, keepdims=True)
        tile = jnp.where((lane == 8) & (row == k), one, tile)
    pairs = lax.dot_general(
        weighted, weighted, (((0,), (0,)), ((), ())), preferred_element_type=jnp.float32
    )
    square = jnp.sum(jnp.sum(pairs * tokgram[...], axis=0, keepdims=True), axis=1, keepdims=True)
    tile = jnp.where((lane == 9) & (row == 0), square, tile)

    for i, nb in enumerate((tnb, xnb, ynb)):
        cur[i] = tile
        copy = pltpu.make_async_remote_copy(
            cur.at[i], got.at[i], red_send.at[i], red_recv.at[i], device_id=nb, device_id_type=MESH
        )
        copy.start()
        copy.wait()
        tile = tile + got[i]
    zslots[mz] = tile
    for shift in (1, 2, 3):
        pltpu.make_async_remote_copy(
            zslots.at[mz], zslots.at[mz], red_send.at[2 + shift], red_recv.at[2 + shift],
            device_id=znb(shift), device_id_type=MESH,
        ).start()
    for shift in (1, 2, 3):
        z = lax.rem(mz + 4 - shift, 4)
        copy = pltpu.make_async_remote_copy(
            zslots.at[mz], zslots.at[z], red_send.at[2 + shift], red_recv.at[2 + shift],
            device_id=znb(shift), device_id_type=MESH,
        )
        copy.wait_recv()
        copy.wait_send()
    total = (zslots[0] + zslots[1]) + (zslots[2] + zslots[3])

    count = float(D * FFW)
    tokens = float(target_ref.shape[1])

    def over(x):
        return jnp.sum(x, axis=1, keepdims=True)

    def down(x):
        return jnp.sum(x, axis=0, keepdims=True)

    gm = jnp.where(lane < kb, total, 0.0) / count
    p_col = over(jnp.where(lane == 8, total, 0.0)) / (count * tokens)
    total_sq = down(over(jnp.where((lane == 9) & (row == 0), total, 0.0))) / (
        count * tokens * tokens
    )
    p_row = down(jnp.where(row == lane, p_col, 0.0))
    c_row = p_row + (p_row - down(gm * p_col))
    c_col = over(jnp.where(row == lane, c_row, 0.0))
    squares = total_sq - 2.0 * over(c_row * p_row) + over(c_row * down(gm * c_col))
    beta = jnp.sqrt(squares)
    coef_out[0:8] = jnp.where(lane == 0, c_col / beta, c_col)
    coef_out[8:16] = jnp.where(row == 0, 1.0 / (beta * tokens), beta)

    @pl.loop(0, steps)
    def _(t):
        copy_out(t).wait()
        for shift in (1, 2, 3):
            copy_z(t, shift, False).wait_send()
        for way in (0, 1):
            copy_2(t, way, False).wait_send()
            copy_3(t, way, False).wait_send()


def finish_kernel(coef, weighted, act, basis, out, hess, field):
    kb = basis.shape[0]
    field[...] = jnp.dot(weighted[...], act[...], preferred_element_type=jnp.float32)
    scale = coef[8, 0]

    @pl.loop(0, out.shape[0] // 16)
    def _(g):
        at = pl.ds(pl.multiple_of(g * 16, 16), 16)
        acc = field[at, :] * scale
        for k in range(kb):
            acc = acc - coef[k, 0] * basis[k, at, :].astype(jnp.float32)
        out[at, :] = acc

    for k in range(kb):
        hess[k] = coef[k, 1]
    hess[kb] = coef[9, 0]


def kernel_body(activations, down_weight, basis, target):
    kb, rows, hidden = basis.shape
    own_tokens = activations.shape[0]
    tokens = target.shape[1]
    steps = hidden // CHUNK
    f32, bf16 = jnp.float32, jnp.bfloat16
    any_spec = pl.BlockSpec(memory_space=pl.ANY)
    vmem = pl.BlockSpec(memory_space=pltpu.VMEM)
    dma = pltpu.SemaphoreType.DMA
    act, weighted, coef = pl.pallas_call(
        functools.partial(gather_kernel, steps),
        out_shape=(
            jax.ShapeDtypeStruct((4, 2, 2, own_tokens, hidden), bf16),
            jax.ShapeDtypeStruct((rows, tokens), bf16),
            jax.ShapeDtypeStruct((16, 128), f32),
        ),
        in_specs=[any_spec, any_spec, any_spec, vmem],
        out_specs=(any_spec, vmem, vmem),
        scratch_shapes=[
            pltpu.VMEM((kb + 1, rows, hidden), bf16),
            pltpu.VMEM((4, 2, 2, own_tokens, hidden), bf16),
            pltpu.VMEM((kb + 1, rows, tokens), f32),
            pltpu.VMEM((kb * GROUP, kb * GROUP), f32),
            pltpu.VMEM((tokens, tokens), f32),
            pltpu.VMEM((2, rows, tokens), f32),
            pltpu.VMEM((3, 8, 128), f32),
            pltpu.VMEM((3, 8, 128), f32),
            pltpu.VMEM((4, 8, 128), f32),
            dma, dma((steps,)), dma((steps,)),
            dma((steps, 3)), dma((steps, 3)),
            dma((2, steps)), dma((2, steps)), dma((2, steps)), dma((2, steps)),
            dma((steps,)),
            dma((2,)), dma((2,)), dma((6,)), dma((6,)),
        ],
        compiler_params=pltpu.CompilerParams(
            collective_id=0, has_side_effects=True, vmem_limit_bytes=62 * 1024 * 1024
        ),
    )(activations, down_weight, basis, target)
    act = act.reshape(tokens, hidden)
    return pl.pallas_call(
        finish_kernel,
        grid=(steps,),
        out_shape=(
            jax.ShapeDtypeStruct((rows, hidden), f32),
            jax.ShapeDtypeStruct((kb + 1,), f32),
        ),
        in_specs=[
            pl.BlockSpec(memory_space=pltpu.SMEM),
            pl.BlockSpec((rows, tokens), lambda i: (0, 0)),
            pl.BlockSpec((tokens, CHUNK), lambda i: (0, i)),
            pl.BlockSpec((kb, rows, CHUNK), lambda i: (0, 0, i)),
        ],
        out_specs=(
            pl.BlockSpec((rows, CHUNK), lambda i: (0, i)),
            pl.BlockSpec(memory_space=pltpu.SMEM),
        ),
        scratch_shapes=[pltpu.VMEM((rows, CHUNK), f32)],
        compiler_params=pltpu.CompilerParams(vmem_limit_bytes=48 * 1024 * 1024),
    )(coef, weighted, act, basis)


def solution(mesh):
    fits = mesh.shape["fsdp"] == 16 and mesh.shape["tp"] == 2
    return jax.shard_map(
        kernel_body if fits else plain_body,
        mesh=mesh,
        in_specs=(P("fsdp", "tp"), P("fsdp", "tp"), P(None, "fsdp", "tp"), P("fsdp", None)),
        out_specs=(P("fsdp", "tp"), P()),
        check_vma=False,
    )
```

```python
import functools
import jax
import jax.numpy as jnp
from jax import lax
from jax.experimental import pallas as pl
from jax.experimental.pallas import tpu as pltpu
from jax.sharding import PartitionSpec as P

D = 4608
FFW = 18432
MESH = pl.DeviceIdType.MESH
NT = (((1,), (1,)), ((), ()))
CHUNK = 1024
HALF = CHUNK // 2
GROUP = 32
LAG = 2


def plain_body(activations, down_weight, basis, target):
    count = float(D * FFW)
    total_tokens = target.shape[1]
    local_rows = down_weight.shape[0]
    basis_count = basis.shape[0]
    basis_flat = basis.reshape(basis_count, -1)
    gram = (
        lax.psum(
            lax.dot_general(
                basis_flat, basis_flat, (((1,), (1,)), ((), ())), preferred_element_type=jnp.float32
            ),
            ("fsdp", "tp"),
        )
        / count
    )
    both = jnp.concatenate([down_weight, basis[basis_count - 1]], 0)
    proj = lax.dot_general(
        both,
        lax.all_gather(activations, "fsdp", axis=0, tiled=True),
        (((1,), (1,)), ((), ())),
        preferred_element_type=jnp.float32,
    )
    summed = lax.psum(proj, "tp")
    slope = jnp.tanh(summed[:local_rows] - target.astype(jnp.float32))
    weighted = ((1.0 - slope * slope) * summed[local_rows:]).astype(jnp.bfloat16)
    hvp = jnp.dot(
        weighted,
        lax.all_gather(activations, "fsdp", axis=0, tiled=True),
        preferred_element_type=jnp.float32,
    ) / float(total_tokens)
    flat = hvp.reshape(1, -1)
    upper = flat.astype(jnp.bfloat16)
    lower = (flat - upper.astype(jnp.float32)).astype(jnp.bfloat16)
    panel = jnp.concatenate([upper, lower], 0)
    pairs = lax.dot_general(
        basis_flat, panel, (((1,), (1,)), ((), ())), preferred_element_type=jnp.float32
    )
    products, total_sq = lax.psum((jnp.sum(pairs, axis=1), jnp.sum(hvp * hvp)), ("fsdp", "tp"))
    products = products / count
    total_sq = total_sq / count
    second = products - jnp.dot(gram, products, precision=lax.Precision.HIGHEST)
    coeffs = products + second
    result = hvp
    for index in range(basis_count):
        result = result - coeffs[index] * basis[index].astype(jnp.float32)
    squares = (
        total_sq
        - 2.0 * jnp.sum(coeffs * products)
        + jnp.sum(coeffs * jnp.dot(gram, coeffs, precision=lax.Precision.HIGHEST))
    )
    beta = jnp.sqrt(squares)
    new_vector = result / beta
    hessenberg = jnp.concatenate([products + second, beta[None]])
    return (new_vector, hessenberg)


def gather_kernel(
    steps, act_hbm, w_hbm, basis_hbm, target_ref,
    act_out, weighted_out, coef_out,
    stack, held, proj, gram, tokgram, other, cube, zslots,
    own_sem, load_w, load_b, z_send, z_recv, s2, r2, s3, r3, out_sem,
    ex_send, ex_recv, cube_send, cube_recv, red_send, red_recv,
):
    me = lax.axis_index("fsdp")
    core = lax.axis_index("tp")
    mz, my, mx = me // 4, (me // 2) % 2, me % 2
    xnb = {"fsdp": mz * 4 + my * 2 + (1 - mx)}
    ynb = {"fsdp": mz * 4 + (1 - my) * 2 + mx}
    tnb = {"tp": 1 - core}
    rows = w_hbm.shape[0]
    kb = basis_hbm.shape[0]

    def cnb(d):
        y, x = (1 - my) if d & 4 else my, (1 - mx) if d & 2 else mx
        c = (1 - core) if d & 1 else core
        return (mz * 4 + y * 2 + x, c), y * 4 + x * 2 + c

    def copy_cube(d, arriving):
        device, theirs = cnb(d)
        slot = cube.at[theirs if arriving else my * 4 + mx * 2 + core]
        return pltpu.make_async_remote_copy(
            slot, slot, cube_send.at[d - 1], cube_recv.at[d - 1],
            device_id=device, device_id_type=MESH,
        )

    def znb(shift):
        return {"fsdp": lax.rem(mz + shift, 4) * 4 + my * 2 + mx}

    def cols(t, start=0, size=CHUNK):
        return pl.ds(pl.multiple_of(t * CHUNK + start, HALF), size)

    own = pltpu.make_async_copy(act_hbm, held.at[mz, my, mx], own_sem)
    own.start()

    def copy_w(t):
        return pltpu.make_async_copy(w_hbm.at[:, cols(t)], stack.at[0, :, cols(t)], load_w.at[t])

    def copy_b(t):
        return pltpu.make_async_copy(
            basis_hbm.at[:, :, cols(t)], stack.at[pl.ds(1, kb), :, cols(t)], load_b.at[t]
        )

    @pl.loop(0, steps)
    def _(t):
        copy_w(t).start()
        copy_b(t).start()

    barrier = pltpu.get_barrier_semaphore()
    for nb in [znb(1), znb(2), znb(3)] + [cnb(d)[0] for d in range(1, 8)]:
        pl.semaphore_signal(barrier, inc=1, device_id=nb, device_id_type=MESH)
    proj[...] = jnp.zeros_like(proj)
    gram[...] = jnp.zeros_like(gram)
    tokgram[...] = jnp.zeros_like(tokgram)
    pl.semaphore_wait(barrier, 10)
    own.wait()

    def copy_z(t, shift, arriving):
        z = lax.rem(mz + 4 - shift, 4) if arriving else mz
        part = held.at[z, my, mx, :, cols(t)]
        return pltpu.make_async_remote_copy(
            part, part, z_send.at[t, shift - 1], z_recv.at[t, shift - 1],
            device_id=znb(shift), device_id_type=MESH,
        )

    def copy_2(t, way, arriving):
        if way == 0:
            part = held.at[:, my, (1 - mx) if arriving else mx, :, cols(t, 0, HALF)]
        else:
            part = held.at[:, (1 - my) if arriving else my, mx, :, cols(t, HALF, HALF)]
        return pltpu.make_async_remote_copy(
            part, part, s2.at[way, t], r2.at[way, t],
            device_id=xnb if way == 0 else ynb, device_id_type=MESH,
        )

    def copy_3(t, way, arriving):
        if way == 0:
            part = held.at[:, (1 - my) if arriving else my, :, :, cols(t, 0, HALF)]
        else:
            part = held.at[:, :, (1 - mx) if arriving else mx, :, cols(t, HALF, HALF)]
        return pltpu.make_async_remote_copy(
            part, part, s3.at[way, t], r3.at[way, t],
            device_id=ynb if way == 0 else xnb, device_id_type=MESH,
        )

    def copy_out(t):
        return pltpu.make_async_copy(
            held.at[:, :, :, :, cols(t)], act_out.at[:, :, :, :, cols(t)], out_sem.at[t]
        )

    @pl.loop(0, steps)
    def _(t):
        for shift in (1, 2, 3):
            copy_z(t, shift, False).start()

    @pl.loop(0, steps + 2 * LAG)
    def _(t):
        @pl.when(t < steps)
        def _():
            for shift in (1, 2, 3):
                copy_z(t, shift, True).wait_recv()
            copy_2(t, 0, False).start()
            copy_2(t, 1, False).start()

        @pl.when((t >= LAG) & (t < steps + LAG))
        def _():
            u = t - LAG
            for way in (0, 1):
                copy_2(u, way, True).wait_recv()
                copy_3(u, way, False).start()

        @pl.when(t < steps)
        def _():
            copy_w(t).wait()
            copy_b(t).wait()

            @pl.loop(0, rows // GROUP)
            def _(g):
                at = pl.ds(pl.multiple_of(g * GROUP, GROUP), GROUP)
                part = stack[1:, at, cols(t)].reshape(kb * GROUP, CHUNK)
                gram[...] += lax.dot_general(part, part, NT, preferred_element_type=jnp.float32)

        @pl.when(t >= 2 * LAG)
        def _():
            u = t - 2 * LAG
            copy_3(u, 0, True).wait_recv()
            copy_3(u, 1, True).wait_recv()
            copy_out(u).start()
            act = held[:, :, :, :, cols(u)].reshape(proj.shape[2], CHUNK)
            tokgram[...] += lax.dot_general(act, act, NT, preferred_element_type=jnp.float32)

            part = stack[:, :, cols(u)].reshape((kb + 1) * rows, CHUNK)
            made = lax.dot_general(part, act, NT, preferred_element_type=jnp.float32)
            proj[...] += made.reshape(kb + 1, rows, proj.shape[2])

    exchange = [
        pltpu.make_async_remote_copy(
            proj.at[k], other.at[i], ex_send.at[i], ex_recv.at[i],
            device_id=tnb, device_id_type=MESH,
        )
        for i, k in enumerate((0, kb))
    ]
    for copy in exchange:
        copy.start()

    lane = lax.broadcasted_iota(jnp.int32, (8, 128), 1)
    row = lax.broadcasted_iota(jnp.int32, (8, 128), 0)
    size = kb * GROUP
    r_at = lax.broadcasted_iota(jnp.int32, (size, size), 0)
    c_at = lax.broadcasted_iota(jnp.int32, (size, size), 1)
    kept = jnp.where(r_at % GROUP == c_at % GROUP, gram[...], 0.0)
    sums = jnp.sum(kept.reshape(kb, GROUP, size), axis=1)
    block = lax.broadcasted_iota(jnp.int32, (kb, size), 1) // GROUP
    tile = jnp.zeros((8, 128), jnp.float32)
    for k in range(kb):
        one = jnp.sum(jnp.where(block == k, sums, 0.0), axis=1, keepdims=True)
        tile = jnp.where(lane == k, one, tile)

    for copy in exchange:
        copy.wait()
    slope = jnp.tanh(proj[0] + other[0] - target_ref[...].astype(jnp.float32))
    weighted = ((1.0 - slope * slope) * (proj[kb] + other[1])).astype(jnp.bfloat16)
    weighted_out[...] = weighted
    wide = weighted.astype(jnp.float32)
    for k in range(kb):
        one = jnp.sum(jnp.sum(wide * proj[k + 1], axis=0, keepdims=True), axis=1, keepdims=True)
        tile = jnp.where((lane == 8) & (row == k), one, tile)
    pairs = lax.dot_general(
        weighted, weighted, (((0,), (0,)), ((), ())), preferred_element_type=jnp.float32
    )
    square = jnp.sum(jnp.sum(pairs * tokgram[...], axis=0, keepdims=True), axis=1, keepdims=True)
    tile = jnp.where((lane == 9) & (row == 0), square, tile)

    mine = my * 4 + mx * 2 + core
    cube[mine] = tile
    for d in range(1, 8):
        copy_cube(d, False).start()
    for d in range(1, 8):
        copy_cube(d, True).wait_recv()
        copy_cube(d, False).wait_send()
    tile = jnp.sum(cube[...], axis=0)
    zslots[mz] = tile
    for shift in (1, 2, 3):
        pltpu.make_async_remote_copy(
            zslots.at[mz], zslots.at[mz], red_send.at[shift - 1], red_recv.at[shift - 1],
            device_id=znb(shift), device_id_type=MESH,
        ).start()
    for shift in (1, 2, 3):
        z = lax.rem(mz + 4 - shift, 4)
        copy = pltpu.make_async_remote_copy(
            zslots.at[mz], zslots.at[z], red_send.at[shift - 1], red_recv.at[shift - 1],
            device_id=znb(shift), device_id_type=MESH,
        )
        copy.wait_recv()
        copy.wait_send()
    total = (zslots[0] + zslots[1]) + (zslots[2] + zslots[3])

    count = float(D * FFW)
    tokens = float(target_ref.shape[1])

    def over(x):
        return jnp.sum(x, axis=1, keepdims=True)

    def down(x):
        return jnp.sum(x, axis=0, keepdims=True)

    gm = jnp.where(lane < kb, total, 0.0) / count
    p_col = over(jnp.where(lane == 8, total, 0.0)) / (count * tokens)
    total_sq = down(over(jnp.where((lane == 9) & (row == 0), total, 0.0))) / (
        count * tokens * tokens
    )
    p_row = down(jnp.where(row == lane, p_col, 0.0))
    c_row = p_row + (p_row - down(gm * p_col))
    c_col = over(jnp.where(row == lane, c_row, 0.0))
    squares = total_sq - 2.0 * over(c_row * p_row) + over(c_row * down(gm * c_col))
    beta = jnp.sqrt(squares)
    coef_out[0:8] = jnp.where(lane == 0, c_col / beta, c_col)
    coef_out[8:16] = jnp.where(row == 0, 1.0 / (beta * tokens), beta)

    @pl.loop(0, steps)
    def _(t):
        copy_out(t).wait()
        for shift in (1, 2, 3):
            copy_z(t, shift, False).wait_send()
        for way in (0, 1):
            copy_2(t, way, False).wait_send()
            copy_3(t, way, False).wait_send()


def finish_kernel(coef, weighted, act, basis, out, hess, field):
    kb = basis.shape[0]
    field[...] = jnp.dot(weighted[...], act[...], preferred_element_type=jnp.float32)
    scale = coef[8, 0]

    @pl.loop(0, out.shape[0] // 16)
    def _(g):
        at = pl.ds(pl.multiple_of(g * 16, 16), 16)
        acc = field[at, :] * scale
        for k in range(kb):
            acc = acc - coef[k, 0] * basis[k, at, :].astype(jnp.float32)
        out[at, :] = acc

    for k in range(kb):
        hess[k] = coef[k, 1]
    hess[kb] = coef[9, 0]


def kernel_body(activations, down_weight, basis, target):
    kb, rows, hidden = basis.shape
    own_tokens = activations.shape[0]
    tokens = target.shape[1]
    steps = hidden // CHUNK
    f32, bf16 = jnp.float32, jnp.bfloat16
    any_spec = pl.BlockSpec(memory_space=pl.ANY)
    vmem = pl.BlockSpec(memory_space=pltpu.VMEM)
    dma = pltpu.SemaphoreType.DMA
    act, weighted, coef = pl.pallas_call(
        functools.partial(gather_kernel, steps),
        out_shape=(
            jax.ShapeDtypeStruct((4, 2, 2, own_tokens, hidden), bf16),
            jax.ShapeDtypeStruct((rows, tokens), bf16),
            jax.ShapeDtypeStruct((16, 128), f32),
        ),
        in_specs=[any_spec, any_spec, any_spec, vmem],
        out_specs=(any_spec, vmem, vmem),
        scratch_shapes=[
            pltpu.VMEM((kb + 1, rows, hidden), bf16),
            pltpu.VMEM((4, 2, 2, own_tokens, hidden), bf16),
            pltpu.VMEM((kb + 1, rows, tokens), f32),
            pltpu.VMEM((kb * GROUP, kb * GROUP), f32),
            pltpu.VMEM((tokens, tokens), f32),
            pltpu.VMEM((2, rows, tokens), f32),
            pltpu.VMEM((8, 8, 128), f32),
            pltpu.VMEM((4, 8, 128), f32),
            dma, dma((steps,)), dma((steps,)),
            dma((steps, 3)), dma((steps, 3)),
            dma((2, steps)), dma((2, steps)), dma((2, steps)), dma((2, steps)),
            dma((steps,)),
            dma((2,)), dma((2,)), dma((7,)), dma((7,)), dma((3,)), dma((3,)),
        ],
        compiler_params=pltpu.CompilerParams(
            collective_id=0, has_side_effects=True, vmem_limit_bytes=62 * 1024 * 1024
        ),
    )(activations, down_weight, basis, target)
    act = act.reshape(tokens, hidden)
    return pl.pallas_call(
        finish_kernel,
        grid=(steps,),
        out_shape=(
            jax.ShapeDtypeStruct((rows, hidden), f32),
            jax.ShapeDtypeStruct((kb + 1,), f32),
        ),
        in_specs=[
            pl.BlockSpec(memory_space=pltpu.SMEM),
            pl.BlockSpec((rows, tokens), lambda i: (0, 0)),
            pl.BlockSpec((tokens, CHUNK), lambda i: (0, i)),
            pl.BlockSpec((kb, rows, CHUNK), lambda i: (0, 0, i)),
        ],
        out_specs=(
            pl.BlockSpec((rows, CHUNK), lambda i: (0, i)),
            pl.BlockSpec(memory_space=pltpu.SMEM),
        ),
        scratch_shapes=[pltpu.VMEM((rows, CHUNK), f32)],
        compiler_params=pltpu.CompilerParams(vmem_limit_bytes=62 * 1024 * 1024),
    )(coef, weighted, act, basis)


def solution(mesh):
    fits = mesh.shape["fsdp"] == 16 and mesh.shape["tp"] == 2
    return jax.shard_map(
        kernel_body if fits else plain_body,
        mesh=mesh,
        in_specs=(P("fsdp", "tp"), P("fsdp", "tp"), P(None, "fsdp", "tp"), P("fsdp", None)),
        out_specs=(P("fsdp", "tp"), P()),
        check_vma=False,
    )
```

```python
import functools
import jax
import jax.numpy as jnp
from jax import lax
from jax.experimental import pallas as pl
from jax.experimental.pallas import tpu as pltpu
from jax.sharding import PartitionSpec as P

D = 4608
FFW = 18432
MESH = pl.DeviceIdType.MESH
NT = (((1,), (1,)), ((), ()))
CHUNK = 1024
HALF = CHUNK // 2
GROUP = 32
WIDE = 2304
LAG = 2


def plain_body(activations, down_weight, basis, target):
    count = float(D * FFW)
    total_tokens = target.shape[1]
    local_rows = down_weight.shape[0]
    basis_count = basis.shape[0]
    basis_flat = basis.reshape(basis_count, -1)
    gram = (
        lax.psum(
            lax.dot_general(
                basis_flat, basis_flat, (((1,), (1,)), ((), ())), preferred_element_type=jnp.float32
            ),
            ("fsdp", "tp"),
        )
        / count
    )
    both = jnp.concatenate([down_weight, basis[basis_count - 1]], 0)
    proj = lax.dot_general(
        both,
        lax.all_gather(activations, "fsdp", axis=0, tiled=True),
        (((1,), (1,)), ((), ())),
        preferred_element_type=jnp.float32,
    )
    summed = lax.psum(proj, "tp")
    slope = jnp.tanh(summed[:local_rows] - target.astype(jnp.float32))
    weighted = ((1.0 - slope * slope) * summed[local_rows:]).astype(jnp.bfloat16)
    hvp = jnp.dot(
        weighted,
        lax.all_gather(activations, "fsdp", axis=0, tiled=True),
        preferred_element_type=jnp.float32,
    ) / float(total_tokens)
    flat = hvp.reshape(1, -1)
    upper = flat.astype(jnp.bfloat16)
    lower = (flat - upper.astype(jnp.float32)).astype(jnp.bfloat16)
    panel = jnp.concatenate([upper, lower], 0)
    pairs = lax.dot_general(
        basis_flat, panel, (((1,), (1,)), ((), ())), preferred_element_type=jnp.float32
    )
    products, total_sq = lax.psum((jnp.sum(pairs, axis=1), jnp.sum(hvp * hvp)), ("fsdp", "tp"))
    products = products / count
    total_sq = total_sq / count
    second = products - jnp.dot(gram, products, precision=lax.Precision.HIGHEST)
    coeffs = products + second
    result = hvp
    for index in range(basis_count):
        result = result - coeffs[index] * basis[index].astype(jnp.float32)
    squares = (
        total_sq
        - 2.0 * jnp.sum(coeffs * products)
        + jnp.sum(coeffs * jnp.dot(gram, coeffs, precision=lax.Precision.HIGHEST))
    )
    beta = jnp.sqrt(squares)
    new_vector = result / beta
    hessenberg = jnp.concatenate([products + second, beta[None]])
    return (new_vector, hessenberg)


def gather_kernel(
    steps, act_hbm, w_hbm, basis_hbm, target_ref,
    act_out, weighted_out, coef_out,
    stack, held, proj, gram, tokgram, other, cube, zslots,
    own_sem, load_w, load_b, z_send, z_recv, s2, r2, s3, r3, out_sem,
    ex_send, ex_recv, cube_send, cube_recv, red_send, red_recv,
):
    me = lax.axis_index("fsdp")
    core = lax.axis_index("tp")
    mz, my, mx = me // 4, (me // 2) % 2, me % 2
    xnb = {"fsdp": mz * 4 + my * 2 + (1 - mx)}
    ynb = {"fsdp": mz * 4 + (1 - my) * 2 + mx}
    tnb = {"tp": 1 - core}
    rows = w_hbm.shape[0]
    kb = basis_hbm.shape[0]

    def cnb(d):
        y, x = (1 - my) if d & 4 else my, (1 - mx) if d & 2 else mx
        c = (1 - core) if d & 1 else core
        return (mz * 4 + y * 2 + x, c), y * 4 + x * 2 + c

    def copy_cube(d, arriving):
        device, theirs = cnb(d)
        slot = cube.at[theirs if arriving else my * 4 + mx * 2 + core]
        return pltpu.make_async_remote_copy(
            slot, slot, cube_send.at[d - 1], cube_recv.at[d - 1],
            device_id=device, device_id_type=MESH,
        )

    def znb(shift):
        return {"fsdp": lax.rem(mz + shift, 4) * 4 + my * 2 + mx}

    def cols(t, start=0, size=CHUNK):
        return pl.ds(pl.multiple_of(t * CHUNK + start, HALF), size)

    own = pltpu.make_async_copy(act_hbm, held.at[mz, my, mx], own_sem)
    own.start()

    def copy_w(t):
        return pltpu.make_async_copy(w_hbm.at[:, cols(t)], stack.at[0, :, cols(t)], load_w.at[t])

    def copy_b(t):
        return pltpu.make_async_copy(
            basis_hbm.at[:, :, cols(t)], stack.at[pl.ds(1, kb), :, cols(t)], load_b.at[t]
        )

    @pl.loop(0, steps)
    def _(t):
        copy_w(t).start()
        copy_b(t).start()

    barrier = pltpu.get_barrier_semaphore()
    for nb in [znb(1), znb(2), znb(3)] + [cnb(d)[0] for d in range(1, 8)]:
        pl.semaphore_signal(barrier, inc=1, device_id=nb, device_id_type=MESH)
    proj[...] = jnp.zeros_like(proj)
    gram[...] = jnp.zeros_like(gram)
    tokgram[...] = jnp.zeros_like(tokgram)
    pl.semaphore_wait(barrier, 10)
    own.wait()

    def copy_z(t, shift, arriving):
        z = lax.rem(mz + 4 - shift, 4) if arriving else mz
        part = held.at[z, my, mx, :, cols(t)]
        return pltpu.make_async_remote_copy(
            part, part, z_send.at[t, shift - 1], z_recv.at[t, shift - 1],
            device_id=znb(shift), device_id_type=MESH,
        )

    def copy_2(t, way, arriving):
        if way == 0:
            part = held.at[:, my, (1 - mx) if arriving else mx, :, cols(t, 0, HALF)]
        else:
            part = held.at[:, (1 - my) if arriving else my, mx, :, cols(t, HALF, HALF)]
        return pltpu.make_async_remote_copy(
            part, part, s2.at[way, t], r2.at[way, t],
            device_id=xnb if way == 0 else ynb, device_id_type=MESH,
        )

    def copy_3(t, way, arriving):
        if way == 0:
            part = held.at[:, (1 - my) if arriving else my, :, :, cols(t, 0, HALF)]
        else:
            part = held.at[:, :, (1 - mx) if arriving else mx, :, cols(t, HALF, HALF)]
        return pltpu.make_async_remote_copy(
            part, part, s3.at[way, t], r3.at[way, t],
            device_id=ynb if way == 0 else xnb, device_id_type=MESH,
        )

    def copy_out(t):
        return pltpu.make_async_copy(
            held.at[:, :, :, :, cols(t)], act_out.at[:, :, :, :, cols(t)], out_sem.at[t]
        )

    @pl.loop(0, steps)
    def _(t):
        for shift in (1, 2, 3):
            copy_z(t, shift, False).start()

    @pl.loop(0, steps + 2 * LAG)
    def _(t):
        @pl.when(t < steps)
        def _():
            for shift in (1, 2, 3):
                copy_z(t, shift, True).wait_recv()
            copy_2(t, 0, False).start()
            copy_2(t, 1, False).start()

        @pl.when((t >= LAG) & (t < steps + LAG))
        def _():
            u = t - LAG
            for way in (0, 1):
                copy_2(u, way, True).wait_recv()
                copy_3(u, way, False).start()

        @pl.when(t < steps)
        def _():
            copy_w(t).wait()
            copy_b(t).wait()

            @pl.loop(0, rows // GROUP)
            def _(g):
                at = pl.ds(pl.multiple_of(g * GROUP, GROUP), GROUP)
                part = stack[1:, at, cols(t)].reshape(kb * GROUP, CHUNK)
                gram[...] += lax.dot_general(part, part, NT, preferred_element_type=jnp.float32)

        @pl.when(t >= 2 * LAG)
        def _():
            u = t - 2 * LAG
            copy_3(u, 0, True).wait_recv()
            copy_3(u, 1, True).wait_recv()
            copy_out(u).start()
            act = held[:, :, :, :, cols(u)].reshape(proj.shape[2], CHUNK)
            tokgram[...] += lax.dot_general(act, act, NT, preferred_element_type=jnp.float32)

            part = stack[:, :, cols(u)].reshape((kb + 1) * rows, CHUNK)
            made = lax.dot_general(part, act, NT, preferred_element_type=jnp.float32)
            proj[...] += made.reshape(kb + 1, rows, proj.shape[2])

    exchange = [
        pltpu.make_async_remote_copy(
            proj.at[k], other.at[i], ex_send.at[i], ex_recv.at[i],
            device_id=tnb, device_id_type=MESH,
        )
        for i, k in enumerate((0, kb))
    ]
    for copy in exchange:
        copy.start()

    lane = lax.broadcasted_iota(jnp.int32, (8, 128), 1)
    row = lax.broadcasted_iota(jnp.int32, (8, 128), 0)
    size = kb * GROUP
    r_at = lax.broadcasted_iota(jnp.int32, (size, size), 0)
    c_at = lax.broadcasted_iota(jnp.int32, (size, size), 1)
    kept = jnp.where(r_at % GROUP == c_at % GROUP, gram[...], 0.0)
    sums = jnp.sum(kept.reshape(kb, GROUP, size), axis=1)
    block = lax.broadcasted_iota(jnp.int32, (kb, size), 1) // GROUP
    tile = jnp.zeros((8, 128), jnp.float32)
    for k in range(kb):
        one = jnp.sum(jnp.where(block == k, sums, 0.0), axis=1, keepdims=True)
        tile = jnp.where(lane == k, one, tile)

    for copy in exchange:
        copy.wait()
    slope = jnp.tanh(proj[0] + other[0] - target_ref[...].astype(jnp.float32))
    weighted = ((1.0 - slope * slope) * (proj[kb] + other[1])).astype(jnp.bfloat16)
    weighted_out[...] = weighted
    wide = weighted.astype(jnp.float32)
    for k in range(kb):
        one = jnp.sum(jnp.sum(wide * proj[k + 1], axis=0, keepdims=True), axis=1, keepdims=True)
        tile = jnp.where((lane == 8) & (row == k), one, tile)
    pairs = lax.dot_general(
        weighted, weighted, (((0,), (0,)), ((), ())), preferred_element_type=jnp.float32
    )
    square = jnp.sum(jnp.sum(pairs * tokgram[...], axis=0, keepdims=True), axis=1, keepdims=True)
    tile = jnp.where((lane == 9) & (row == 0), square, tile)

    mine = my * 4 + mx * 2 + core
    cube[mine] = tile
    for d in range(1, 8):
        copy_cube(d, False).start()
    for d in range(1, 8):
        copy_cube(d, True).wait_recv()
        copy_cube(d, False).wait_send()
    tile = jnp.sum(cube[...], axis=0)
    zslots[mz] = tile
    for shift in (1, 2, 3):
        pltpu.make_async_remote_copy(
            zslots.at[mz], zslots.at[mz], red_send.at[shift - 1], red_recv.at[shift - 1],
            device_id=znb(shift), device_id_type=MESH,
        ).start()
    for shift in (1, 2, 3):
        z = lax.rem(mz + 4 - shift, 4)
        copy = pltpu.make_async_remote_copy(
            zslots.at[mz], zslots.at[z], red_send.at[shift - 1], red_recv.at[shift - 1],
            device_id=znb(shift), device_id_type=MESH,
        )
        copy.wait_recv()
        copy.wait_send()
    total = (zslots[0] + zslots[1]) + (zslots[2] + zslots[3])

    count = float(D * FFW)
    tokens = float(target_ref.shape[1])

    def over(x):
        return jnp.sum(x, axis=1, keepdims=True)

    def down(x):
        return jnp.sum(x, axis=0, keepdims=True)

    gm = jnp.where(lane < kb, total, 0.0) / count
    p_col = over(jnp.where(lane == 8, total, 0.0)) / (count * tokens)
    total_sq = down(over(jnp.where((lane == 9) & (row == 0), total, 0.0))) / (
        count * tokens * tokens
    )
    p_row = down(jnp.where(row == lane, p_col, 0.0))
    c_row = p_row + (p_row - down(gm * p_col))
    c_col = over(jnp.where(row == lane, c_row, 0.0))
    squares = total_sq - 2.0 * over(c_row * p_row) + over(c_row * down(gm * c_col))
    beta = jnp.sqrt(squares)
    coef_out[0:8] = jnp.where(lane == 0, c_col / beta, c_col)
    coef_out[8:16] = jnp.where(row == 0, 1.0 / (beta * tokens), beta)

    @pl.loop(0, steps)
    def _(t):
        copy_out(t).wait()
        for shift in (1, 2, 3):
            copy_z(t, shift, False).wait_send()
        for way in (0, 1):
            copy_2(t, way, False).wait_send()
            copy_3(t, way, False).wait_send()


def finish_kernel(coef, weighted, act, basis, out, hess, field):
    kb = basis.shape[0]
    field[...] = jnp.dot(weighted[...], act[...], preferred_element_type=jnp.float32)
    scale = coef[8, 0]

    @pl.loop(0, out.shape[0] // 32)
    def _(g):
        at = pl.ds(pl.multiple_of(g * 32, 32), 32)
        acc = field[at, :] * scale
        for k in range(kb):
            acc = acc - coef[k, 0] * basis[k, at, :].astype(jnp.float32)
        out[at, :] = acc

    for k in range(kb):
        hess[k] = coef[k, 1]
    hess[kb] = coef[9, 0]


def kernel_body(activations, down_weight, basis, target):
    kb, rows, hidden = basis.shape
    own_tokens = activations.shape[0]
    tokens = target.shape[1]
    steps = hidden // CHUNK
    f32, bf16 = jnp.float32, jnp.bfloat16
    any_spec = pl.BlockSpec(memory_space=pl.ANY)
    vmem = pl.BlockSpec(memory_space=pltpu.VMEM)
    dma = pltpu.SemaphoreType.DMA
    act, weighted, coef = pl.pallas_call(
        functools.partial(gather_kernel, steps),
        out_shape=(
            jax.ShapeDtypeStruct((4, 2, 2, own_tokens, hidden), bf16),
            jax.ShapeDtypeStruct((rows, tokens), bf16),
            jax.ShapeDtypeStruct((16, 128), f32),
        ),
        in_specs=[any_spec, any_spec, any_spec, vmem],
        out_specs=(any_spec, vmem, vmem),
        scratch_shapes=[
            pltpu.VMEM((kb + 1, rows, hidden), bf16),
            pltpu.VMEM((4, 2, 2, own_tokens, hidden), bf16),
            pltpu.VMEM((kb + 1, rows, tokens), f32),
            pltpu.VMEM((kb * GROUP, kb * GROUP), f32),
            pltpu.VMEM((tokens, tokens), f32),
            pltpu.VMEM((2, rows, tokens), f32),
            pltpu.VMEM((8, 8, 128), f32),
            pltpu.VMEM((4, 8, 128), f32),
            dma, dma((steps,)), dma((steps,)),
            dma((steps, 3)), dma((steps, 3)),
            dma((2, steps)), dma((2, steps)), dma((2, steps)), dma((2, steps)),
            dma((steps,)),
            dma((2,)), dma((2,)), dma((7,)), dma((7,)), dma((3,)), dma((3,)),
        ],
        compiler_params=pltpu.CompilerParams(
            collective_id=0, has_side_effects=True, vmem_limit_bytes=62 * 1024 * 1024
        ),
    )(activations, down_weight, basis, target)
    act = act.reshape(tokens, hidden)
    return pl.pallas_call(
        finish_kernel,
        grid=(hidden // WIDE,),
        out_shape=(
            jax.ShapeDtypeStruct((rows, hidden), f32),
            jax.ShapeDtypeStruct((kb + 1,), f32),
        ),
        in_specs=[
            pl.BlockSpec(memory_space=pltpu.SMEM),
            pl.BlockSpec((rows, tokens), lambda i: (0, 0)),
            pl.BlockSpec((tokens, WIDE), lambda i: (0, i)),
            pl.BlockSpec((kb, rows, WIDE), lambda i: (0, 0, i)),
        ],
        out_specs=(
            pl.BlockSpec((rows, WIDE), lambda i: (0, i)),
            pl.BlockSpec(memory_space=pltpu.SMEM),
        ),
        scratch_shapes=[pltpu.VMEM((rows, WIDE), f32)],
        compiler_params=pltpu.CompilerParams(vmem_limit_bytes=62 * 1024 * 1024),
    )(coef, weighted, act, basis)


def solution(mesh):
    fits = mesh.shape["fsdp"] == 16 and mesh.shape["tp"] == 2
    return jax.shard_map(
        kernel_body if fits else plain_body,
        mesh=mesh,
        in_specs=(P("fsdp", "tp"), P("fsdp", "tp"), P(None, "fsdp", "tp"), P("fsdp", None)),
        out_specs=(P("fsdp", "tp"), P()),
        check_vma=False,
    )
```
